32 devices in a mesh: section: 2 (over x), expert: 16 (over z, y, core).
Axes of the slice: x: 2, y: 2, z: 4, core: 2. Of those that a mesh axis runs over, the one named last changes fastest.
Arguments:
- out_grad: bfloat16 [2, 512, 2048], P('section', 'expert'), may hold values from -6 to 6
- layer_input: bfloat16 [2, 512, 2048], P('section', 'expert'), may hold values from -6 to 6
- router_weight: bfloat16 [2, 2048, 16], P('section'), may hold values from -0.125 to 0.125
- expert_ids: int32 [2, 512, 8], P('section', 'expert'), may hold values from 0 to 15, all different within a row; in each aligned block of 32 rows (0 to 31, 32 to 63, ..., all dimensions but the last counted through in order) at most 24 rows name the same one
- hidden_act: bfloat16 [2, 16, 384, 384], P('section', 'expert'), may hold values from -6 to 6
- down_weight: bfloat16 [2, 16, 384, 2048], P('section', 'expert'), may hold values from -0.3125 to 0.3125
Outputs:
- sent_grad: bfloat16 [2, 512, 2048], P('section', 'expert')
- hidden_grad: bfloat16 [2, 16, 384, 384], P('section', 'expert')
- router_grad: float32 [2, 2048, 16], P('section', 'expert')
The draws below stay inside these ranges and needn't reach their ends.
Inputs may be any that keep to these rules, and one draw needn't show every extreme that they name: `expert_ids`: each token names 8 different experts. In each aligned block of 32 tokens (the tokens of one device) no expert is named by more than 24 tokens, a bound that some block reaches.
All inputs are finite; a program needn't handle non-finite values.
Results may differ from the reference program's by a relative error of at most 0.0095.
Values may be sent and summed in bfloat16 or wider, within the bound.
A program may use at most 64 MiB of HBM per device.

```python
import math
import jax
import jax.numpy as jnp
import numpy as np
from jax import lax

D = 2048
F = 384
TOPK = 8
TOK_DEV = 32
SECTIONS = 2
EXPERTS = 16
TOKENS = 512
CAP = 24
SLOTS = 384
N_EXPERT = 16


def shard_levels(rng, extent, shards, least, high):
    def one(dim, blocks):
        heights = jax.random.uniform(jax.random.fold_in(jax.random.fold_in(rng, 6), dim), (blocks,), jnp.float32, least / len(shards), high / len(shards))
        return jnp.repeat(jnp.exp(heights), extent[dim] // blocks).reshape((-1,) + (1,) * (len(extent) - dim - 1))

    loudness = one(*shards[0])
    for cut in shards[1:]:
        loudness = loudness * one(*cut)
    return loudness


def assign_block(stream_key, own, number, rows, number_of, top, most, lean):
    ranking = jax.random.permutation(stream_key, number_of)
    crowded, common = portions_of(number_of, rows * top, most, lean, True), portions_of(number_of, rows * top, most, lean, False)
    places = jnp.arange(number_of)

    def named(sizes, rotation):
        used = int((sizes > 0).sum())
        fixed = max(1, used // 4)
        passed = fixed + (places - fixed + rotation * (used - fixed)) % max(1, number_of - fixed)
        return jnp.zeros((number_of,), jnp.int32).at[ranking[jnp.where(places < fixed, places, passed)]].set(jnp.asarray(sizes, jnp.int32))

    sizes = jnp.where(number % 4 == 0, named(crowded, number // 4), named(common, number - number // 4 - 1))
    mixed = jax.random.permutation(jax.random.fold_in(own, 3), number_of)
    giver, taker = mixed[0:number_of // 2 * 2:2], mixed[1:number_of // 2 * 2:2]
    margin = jnp.minimum(sizes[giver] - 1, most - sizes[taker]) // 2
    margin = jnp.where((giver == ranking[0]) | (taker == ranking[0]) | (sizes[taker] == 0), 0, jnp.maximum(margin, 0))
    passed = jax.random.randint(jax.random.fold_in(own, 4), (number_of // 2,), 0, 1 << 20) % (margin + 1)
    sizes = sizes.at[giver].add(-passed).at[taker].add(passed)
    members = jnp.searchsorted(jnp.cumsum(sizes), jnp.arange(rows * top), side="right").astype(jnp.int32)
    listing = members.reshape(top, rows).T
    listing = listing[jax.random.permutation(jax.random.fold_in(own, 1), rows)]
    rotation = jax.random.randint(jax.random.fold_in(own, 2), (rows, 1), 0, top)
    return jnp.take_along_axis(listing, (jnp.arange(top)[None, :] + rotation) % top, axis=1)


def portions_of(number_of, total, limit, slope, full):
    weights = [(1 << 20) // math.isqrt(grade ** slope) + 1 for grade in range(1, number_of + 1)]
    largest = limit if full else min(limit, max(-(-total // number_of), total * weights[0] // sum(weights)))
    least = 1 if total - largest >= number_of - 1 else 0
    given, rest = [largest] + [least] * (number_of - 1), total - largest - least * (number_of - 1)
    while rest > 0:
        movable = [i for i in range(1, number_of) if given[i] < largest] or [i for i in range(1, number_of) if given[i] < limit]
        pool, remaining = sum([weights[i] for i in movable]), rest
        for i in movable:
            more = min(limit - given[i], max(1, remaining * weights[i] // pool), rest)
            given[i] = given[i] + more
            rest = rest - more
    return np.array(given)


def gaussian(own_key, dims, scale, reach, split=(), kind=jnp.bfloat16):
    level = shard_levels(own_key, dims, split, -0.22, 0.18) if split else 1.0
    values = jax.random.normal(own_key, dims, jnp.float32) * scale * level
    return jnp.minimum(jnp.maximum(values, -reach), reach).astype(kind)


def setup_inputs(seed: int = 0) -> dict:
    keys = jax.random.split(jax.random.key(seed), 7)
    out_grad = gaussian(keys[0], (SECTIONS, TOKENS, D), 1.0, 6.0, ((0, 2), (1, 16)))
    layer_input = gaussian(keys[1], (SECTIONS, TOKENS, D), 1.0, 6.0, ((0, 2), (1, 16)))
    router_weight = gaussian(keys[2], (SECTIONS, D, EXPERTS), D ** -0.5, 0.125, ((0, 2),))
    expert_ids_keys = jax.random.split(jax.random.fold_in(keys[3], 1), SECTIONS * TOKENS // TOK_DEV)
    expert_ids_turns = jax.random.permutation(jax.random.fold_in(keys[3], 3), SECTIONS * TOKENS // TOK_DEV)
    expert_ids = jax.vmap(lambda own, number: assign_block(jax.random.fold_in(keys[3], 2), own, number, TOK_DEV, EXPERTS, TOPK, CAP, 2))(expert_ids_keys, expert_ids_turns).reshape((SECTIONS, TOKENS, TOPK))
    hidden_act = gaussian(keys[4], (SECTIONS, EXPERTS, SLOTS, F), 1.0, 6.0, ((0, 2), (1, 16)))
    down_weight = gaussian(keys[5], (SECTIONS, EXPERTS, F, D), F ** -0.5, 0.3125, ((0, 2), (1, 16)))
    return {"out_grad": out_grad, "layer_input": layer_input, "router_weight": router_weight, "expert_ids": expert_ids, "hidden_act": hidden_act, "down_weight": down_weight}


def expert_pass(operands):
    hidden, w_down, dispatched, slot_gates = operands
    expert_out = jnp.dot(hidden, w_down, preferred_element_type=jnp.float32)
    slot_dg = jnp.sum(dispatched.astype(jnp.float32) * expert_out, axis=-1)
    scaled = (slot_gates.astype(jnp.float32)[:, None] * dispatched.astype(jnp.float32)).astype(jnp.bfloat16)
    hidden_grad = jnp.dot(scaled, w_down.T, preferred_element_type=jnp.float32).astype(jnp.bfloat16)
    return slot_dg, hidden_grad


def section_backward(out_grads, inputs, router, chosen_ids, hidden, w_down):
    logits = jnp.dot(inputs, router, preferred_element_type=jnp.float32)
    picked = (chosen_ids[:, :, None] == jnp.arange(EXPERTS, dtype=jnp.int32)[None, None, :]).astype(jnp.float32)
    chosen_logits = jnp.sum(picked * logits[:, None, :], axis=-1)
    weights = jnp.exp(chosen_logits)
    gate_vals = (weights / jnp.sum(weights, axis=-1, keepdims=True)).astype(jnp.bfloat16)
    blocked = picked.reshape(N_EXPERT, TOK_DEV * TOPK, EXPERTS)
    before = jnp.cumsum(blocked, axis=1) - blocked
    slot_rank = jnp.sum(before * blocked, axis=-1).astype(jnp.int32).reshape(TOKENS, TOPK)
    source = (jnp.arange(TOKENS, dtype=jnp.int32) // TOK_DEV)[:, None]
    slot_row = (source * CAP + slot_rank).astype(jnp.int32)
    spread = jnp.broadcast_to(out_grads[:, None, :], (TOKENS, TOPK, D))
    dispatched = jnp.zeros((EXPERTS, SLOTS, D), jnp.bfloat16).at[chosen_ids, slot_row].set(spread)
    slot_gates = jnp.zeros((EXPERTS, SLOTS), jnp.bfloat16).at[chosen_ids, slot_row].set(gate_vals)
    slot_dg, hidden_grad = lax.map(expert_pass, (hidden, w_down, dispatched, slot_gates))
    gate_grad = slot_dg[chosen_ids, slot_row]
    gate_float = gate_vals.astype(jnp.float32)
    dchosen = gate_float * (gate_grad - jnp.sum(gate_float * gate_grad, axis=-1, keepdims=True))
    logit_grad = jnp.sum(dchosen[:, :, None] * picked, axis=1).astype(jnp.bfloat16)
    input_grad = (out_grads.astype(jnp.float32) + jnp.dot(logit_grad, router.T, preferred_element_type=jnp.float32)).astype(jnp.bfloat16)
    router_grad = jnp.dot(inputs.T, logit_grad, preferred_element_type=jnp.float32)
    return input_grad, hidden_grad, router_grad


def reference(out_grad, layer_input, router_weight, expert_ids, hidden_act, down_weight):
    input_list = []
    hidden_list = []
    router_list = []
    for section_index in range(SECTIONS):
        input_grad, hidden_grad, router_grad = section_backward(out_grad[section_index], layer_input[section_index], router_weight[section_index], expert_ids[section_index], hidden_act[section_index], down_weight[section_index])
        input_list.append(input_grad)
        hidden_list.append(hidden_grad)
        router_list.append(router_grad)
    input_all = jnp.stack(input_list, axis=0)
    sent_grad = jnp.roll(input_all, -1, axis=0)
    return sent_grad, jnp.stack(hidden_list, axis=0), jnp.stack(router_list, axis=0)
```

```python
import functools

import jax
import jax.numpy as jnp
from jax import lax
from jax.experimental import pallas as pl
from jax.experimental.pallas import tpu as pltpu
from jax.sharding import PartitionSpec as P

MESH = pl.DeviceIdType.MESH
NT = (((1,), (1,)), ((), ()))
TN = (((0,), (0,)), ((), ()))
NN = (((1,), (0,)), ((), ()))
LANES = 128
ROWS_A = 4
CHUNKS = 2
A_UP, A_DOWN, B_NEXT, B_PREV, SIB = range(5)


def dot(lhs, rhs, dims):
    return lax.dot_general(lhs, rhs, dims, preferred_element_type=jnp.float32)


def kernel(
    sections, n, og, x, rt, ids, hid, w, out_g, out_h, out_r,
    xg, xs, meta, dgb, ogn, rtn, lgn, xv, rtv, idv, hv, wv,
    gt, sel, hs, u, v, dgo, dg2, lg, outv, hgv, rgv,
    blk_recv, blk_send, meta_recv, meta_send, slab_recv, slab_send,
    dg_recv, dg_send, sec_recv, sec_send, loc,
):
    tokens, d_model = og.shape
    topk = ids.shape[0]
    experts = rt.shape[0]
    slots, f_dim = hid.shape
    cap = slots // n
    feats = out_r.shape[1]
    per_tile = LANES // tokens
    tiles = n // per_tile
    nb = n // (2 * ROWS_A)
    tiles_per_group = tiles // ROWS_A
    rows = tokens // CHUNKS

    me = lax.axis_index("expert")
    sec = lax.axis_index("section")
    c = lax.rem(me, 2)
    b = lax.rem(me // 2, nb)
    a = me // (2 * nb)
    sib = me + 1 - 2 * c
    prev = lax.rem(sec + sections - 1, sections)
    nxt = lax.rem(sec + 1, sections)
    tile = me // per_tile
    offset = lax.rem(me, per_tile) * tokens

    local = [
        pltpu.make_async_copy(x, xv, loc.at[0]),
        pltpu.make_async_copy(rt, rtv, loc.at[1]),
        pltpu.make_async_copy(ids, idv, loc.at[2]),
        pltpu.make_async_copy(og, xg.at[me], loc.at[3]),
        pltpu.make_async_copy(w, wv, loc.at[4]),
        pltpu.make_async_copy(hid, hv, loc.at[5]),
    ]
    for copy in local:
        copy.start()

    barrier = pltpu.get_barrier_semaphore()

    def greet(d, carry):
        pl.semaphore_signal(
            barrier, inc=1, device_id={"expert": lax.rem(me + d, n)}, device_id_type=MESH
        )
        return carry

    lax.fori_loop(1, n, greet, 0)
    near = (prev,) if sections == 2 else (prev, nxt)
    for other in near:
        pl.semaphore_signal(barrier, inc=1, device_id={"section": other}, device_id_type=MESH)
    pl.semaphore_wait(barrier, n - 1 + len(near))

    def block_copy(idx, q, target, way, own=False):
        part = pl.ds(q * rows, rows)
        return pltpu.make_async_remote_copy(
            src_ref=og.at[part] if own else xg.at[idx, part],
            dst_ref=xg.at[idx, part],
            send_sem=blk_send.at[idx, q, way],
            recv_sem=blk_recv.at[idx, q],
            device_id={"expert": target},
            device_id_type=MESH,
        )

    def column_sends(g, q, do, own=False):
        idx = (g * nb + b) * 2 + c

        @pl.when(jnp.logical_and(g <= a, a < ROWS_A - 1))
        def _():
            do(block_copy(idx, q, me + 2 * nb, A_UP, own))

        @pl.when(jnp.logical_and(g >= a, a > 0))
        def _():
            do(block_copy(idx, q, me - 2 * nb, A_DOWN, own))

        @pl.when(b < nb - 1)
        def _():
            do(block_copy(idx, q, me + 2, B_NEXT, own))

        @pl.when(b > 0)
        def _():
            do(block_copy(idx, q, me - 2, B_PREV, own))

        do(block_copy(idx, q, sib, SIB, own))

    def cross_sends(g, b2, q, do):
        idx = (g * nb + b2) * 2 + c
        if nb > 2:
            @pl.when(jnp.logical_and(b2 < b, b < nb - 1))
            def _():
                do(block_copy(idx, q, me + 2, B_NEXT))

            @pl.when(jnp.logical_and(b2 > b, b > 0))
            def _():
                do(block_copy(idx, q, me - 2, B_PREV))

        do(block_copy(idx, q, sib, SIB))

    def section_copy(i, src, dst):
        return pltpu.make_async_remote_copy(
            src_ref=src, dst_ref=dst, send_sem=sec_send.at[i], recv_sem=sec_recv.at[i],
            device_id={"section": prev}, device_id_type=MESH,
        )

    grads_over = section_copy(0, og, ogn)
    router_over = section_copy(1, rt, rtn)
    logit_over = section_copy(2, lg.at[tile], lgn)

    def slab_copy(peer):
        lane = pl.multiple_of((peer * feats) // LANES * LANES, LANES)
        return pltpu.make_async_remote_copy(
            src_ref=x.at[:, pl.ds(lane, LANES)], dst_ref=xs.at[me],
            send_sem=slab_send.at[peer], recv_sem=slab_recv.at[me],
            device_id={"expert": peer}, device_id_type=MESH,
        )

    def meta_copy(peer):
        return pltpu.make_async_remote_copy(
            src_ref=meta.at[me], dst_ref=meta.at[me],
            send_sem=meta_send.at[peer], recv_sem=meta_recv.at[me],
            device_id={"expert": peer}, device_id_type=MESH,
        )

    def dg_copy(peer):
        return pltpu.make_async_remote_copy(
            src_ref=dgo, dst_ref=dgb.at[me],
            send_sem=dg_send.at[peer], recv_sem=dg_recv.at[me],
            device_id={"expert": peer}, device_id_type=MESH,
        )

    def await_from(peer, dst, sem):
        pltpu.make_async_remote_copy(
            src_ref=dst, dst_ref=dst, send_sem=sem, recv_sem=sem,
            device_id={"expert": peer}, device_id_type=MESH,
        ).wait_recv()

    def each_peer(fn):
        def step(d, carry):
            fn(lax.rem(me + d, n))
            return carry

        lax.fori_loop(1, n, step, 0)

    start = lambda copy: copy.start()
    finish = lambda copy: copy.wait_send()

    for q in range(CHUNKS):
        column_sends(a, q, start, own=True)
    grads_over.start()
    router_over.start()

    own_lane = pl.multiple_of((me * feats) // LANES * LANES, LANES)
    own_slab = pltpu.make_async_copy(x.at[:, pl.ds(own_lane, LANES)], xs.at[me], loc.at[6])
    own_slab.start()
    for copy in local[:3]:
        copy.wait()
    logits = dot(rtv[...], xv[...], NT)
    row = lax.broadcasted_iota(jnp.int32, (experts, tokens), 0)
    named = row == idv[0:1, :]
    for k in range(1, topk):
        named = jnp.logical_or(named, row == idv[k : k + 1, :])
    weights = jnp.where(named, jnp.exp(logits), 0.0)
    gates = weights / jnp.sum(weights, axis=0, keepdims=True)
    marked = jnp.where(named, gates, -1.0).astype(jnp.bfloat16)
    token_of = lax.broadcasted_iota(jnp.int32, (tokens, LANES), 0)
    lane_of = lax.broadcasted_iota(jnp.int32, (tokens, LANES), 1)
    place = jnp.where(lane_of == token_of + offset, 1.0, 0.0).astype(jnp.bfloat16)
    meta[me] = dot(marked, place, NN).astype(jnp.bfloat16)
    each_peer(lambda peer: meta_copy(peer).start())
    each_peer(lambda peer: slab_copy(peer).start())
    for copy in local[3:]:
        copy.wait()

    def order(k):
        closest = jnp.minimum(a, ROWS_A - 1 - a)
        d = (k + 1) // 2
        both = jnp.where(lax.rem(k, 2) == 1, a - d, a + d)
        rest = jnp.where(a <= ROWS_A - 1 - a, k, ROWS_A - 1 - k)
        return jnp.where(k <= 2 * closest, both, rest)

    def slots_of_expert():
        each_peer(lambda peer: await_from(peer, meta.at[peer], meta_recv.at[peer]))
        erow = lax.broadcasted_iota(jnp.int32, (experts, LANES), 0)
        t_from = lax.broadcasted_iota(jnp.int32, (LANES, LANES), 0)
        t_to = lax.broadcasted_iota(jnp.int32, (LANES, LANES), 1)
        ahead = jnp.where(
            jnp.logical_and(t_from < t_to, t_from // tokens == t_to // tokens), 1.0, 0.0
        ).astype(jnp.bfloat16)
        lane_block = lax.broadcasted_iota(jnp.int32, (1, LANES), 1) // tokens
        slot_row = lax.broadcasted_iota(jnp.int32, (slots, LANES), 0)
        for j in range(tiles):
            total = meta[j * per_tile].astype(jnp.float32)
            for i in range(1, per_tile):
                total = total + meta[j * per_tile + i].astype(jnp.float32)
            gt[j] = total
            mine = jnp.sum(jnp.where(erow == me, total, 0.0), axis=0, keepdims=True)
            taken = jnp.where(mine >= 0.0, 1.0, 0.0)
            many = jnp.broadcast_to(taken, (16, LANES)).astype(jnp.bfloat16)
            rank = dot(many, ahead, NN)[0:1, :].astype(jnp.int32)
            slot = (lane_block + j * per_tile) * cap + rank
            slot = jnp.where(mine >= 0.0, slot, -1)
            hot = jnp.where(slot_row == slot, 1.0, 0.0).astype(jnp.bfloat16)
            sel[:, j * LANES : (j + 1) * LANES] = hot
            hs[j] = dot(hv[...], hot, TN)

    def step(k, carry):
        @pl.when(k < ROWS_A - 1)
        def _():
            g = order(k + 1)
            idx = (g * nb + b) * 2 + c
            for q in range(CHUNKS):
                block_copy(idx, q, sib, SIB).wait_recv()
                column_sends(g, q, start)

        g = order(k)
        for j in range(1, nb):
            b2 = lax.rem(b + j, nb)
            idx = (g * nb + b2) * 2 + c
            for q in range(CHUNKS):
                block_copy(idx, q, sib, SIB).wait_recv()
                cross_sends(g, b2, q, start)
        for b2 in range(nb):
            idx = (g * nb + b2) * 2 + 1 - c
            for q in range(CHUNKS):
                block_copy(idx, q, sib, SIB).wait_recv()

        @pl.when(k == ROWS_A - 2)
        def _():
            slots_of_expert()

        for i in range(tiles_per_group):
            t = g * tiles_per_group + i
            u[t] = dot(
                wv[...], xg[pl.ds(t * per_tile, per_tile)].reshape(LANES, d_model), NT
            )
        return carry

    lax.fori_loop(0, ROWS_A, step, 0)

    for j in range(tiles):
        dgo[j : j + 1, :] = jnp.sum(u[j] * hs[j], axis=0, keepdims=True)
    each_peer(lambda peer: dg_copy(peer).start())

    erow = lax.broadcasted_iota(jnp.int32, (experts, LANES), 0)
    for j in range(tiles):
        mine = jnp.sum(jnp.where(erow == me, gt[j], 0.0), axis=0, keepdims=True)
        v[:, j * LANES : (j + 1) * LANES] = (u[j] * jnp.maximum(mine, 0.0)).astype(jnp.bfloat16)
    hgv[...] = dot(sel[...], v[...], NT).astype(jnp.bfloat16)
    hidden_out = pltpu.make_async_copy(hgv, out_h, loc.at[7])
    hidden_out.start()

    own_slab.wait()
    each_peer(lambda peer: await_from(peer, xs.at[peer], slab_recv.at[peer]))
    grads_over.wait_recv()
    router_over.wait_recv()

    for j in range(tiles):
        dg2[j, pl.ds(me, 1), :] = dgo[j : j + 1, :]

    def take(peer):
        await_from(peer, dgb.at[peer], dg_recv.at[peer])
        for j in range(tiles):
            dg2[j, pl.ds(peer, 1), :] = dgb[peer, j : j + 1, :]

    each_peer(take)
    for j in range(tiles):
        g = jnp.maximum(gt[j], 0.0)
        d = dg2[j]
        lg[j] = (g * (d - jnp.sum(g * d, axis=0, keepdims=True))).astype(jnp.bfloat16)
    logit_over.start()

    lg_all = jnp.concatenate([lg[j] for j in range(tiles)], axis=1)
    part = dot(lg_all, xs[...].reshape(n * tokens, LANES), NN)
    if feats < LANES:
        shift = lax.rem(LANES - lax.rem(me * feats, LANES), LANES)
        part = pltpu.roll(part, shift, 1)[:, :feats]
    rgv[...] = part
    router_out = pltpu.make_async_copy(rgv, out_r, loc.at[8])
    router_out.start()

    logit_over.wait_recv()
    mine = dot(place, lgn[...], NT).astype(jnp.bfloat16)
    outv[...] = (ogn[...].astype(jnp.float32) + dot(mine, rtn[...], NN)).astype(jnp.bfloat16)
    grads_out = pltpu.make_async_copy(outv, out_g, loc.at[9])
    grads_out.start()

    for q in range(CHUNKS):
        column_sends(a, q, finish, own=True)

    def drain(k, carry):
        g = order(k)

        @pl.when(k > 0)
        def _():
            for q in range(CHUNKS):
                column_sends(g, q, finish)

        for j in range(1, nb):
            for q in range(CHUNKS):
                cross_sends(g, lax.rem(b + j, nb), q, finish)
        return carry

    lax.fori_loop(0, ROWS_A, drain, 0)

    def sent(peer):
        meta_copy(peer).wait_send()
        slab_copy(peer).wait_send()
        dg_copy(peer).wait_send()

    each_peer(sent)
    grads_over.wait_send()
    router_over.wait_send()
    logit_over.wait_send()
    hidden_out.wait()
    router_out.wait()
    grads_out.wait()


def shards(sections, n, out_grad, layer_input, router_weight, expert_ids, hidden_act, down_weight):
    og, x, hid, w = out_grad[0], layer_input[0], hidden_act[0, 0], down_weight[0, 0]
    rt, ids = router_weight[0].T, expert_ids[0].T
    tokens, d_model = og.shape
    experts, topk = rt.shape[0], ids.shape[0]
    slots, f_dim = hid.shape
    feats = d_model // n
    total = n * tokens
    tiles = total // LANES
    bf16, f32 = jnp.bfloat16, jnp.float32
    dma = pltpu.SemaphoreType.DMA
    hbm = pl.BlockSpec(memory_space=pl.ANY)
    grads, hidden, router = pl.pallas_call(
        functools.partial(kernel, sections, n),
        out_shape=(
            jax.ShapeDtypeStruct((tokens, d_model), bf16),
            jax.ShapeDtypeStruct((slots, f_dim), bf16),
            jax.ShapeDtypeStruct((experts, feats), f32),
        ),
        in_specs=[hbm] * 6,
        out_specs=(hbm,) * 3,
        scratch_shapes=[
            pltpu.VMEM((n, tokens, d_model), bf16),
            pltpu.VMEM((n, tokens, LANES), bf16),
            pltpu.VMEM((n, experts, LANES), bf16),
            pltpu.VMEM((n, tiles, LANES), f32),
            pltpu.VMEM((tokens, d_model), bf16),
            pltpu.VMEM((experts, d_model), bf16),
            pltpu.VMEM((experts, LANES), bf16),
            pltpu.VMEM((tokens, d_model), bf16),
            pltpu.VMEM((experts, d_model), bf16),
            pltpu.VMEM((topk, tokens), jnp.int32),
            pltpu.VMEM((slots, f_dim), bf16),
            pltpu.VMEM((f_dim, d_model), bf16),
            pltpu.VMEM((tiles, experts, LANES), f32),
            pltpu.VMEM((slots, total), bf16),
            pltpu.VMEM((tiles, f_dim, LANES), f32),
            pltpu.VMEM((tiles, f_dim, LANES), f32),
            pltpu.VMEM((f_dim, total), bf16),
            pltpu.VMEM((tiles, LANES), f32),
            pltpu.VMEM((tiles, experts, LANES), f32),
            pltpu.VMEM((tiles, experts, LANES), bf16),
            pltpu.VMEM((tokens, d_model), bf16),
            pltpu.VMEM((slots, f_dim), bf16),
            pltpu.VMEM((experts, feats), f32),
            dma((n, CHUNKS)),
            dma((n, CHUNKS, 5)),
            dma((n,)),
            dma((n,)),
            dma((n,)),
            dma((n,)),
            dma((n,)),
            dma((n,)),
            dma((3,)),
            dma((3,)),
            dma((10,)),
        ],
        compiler_params=pltpu.CompilerParams(
            collective_id=0, has_side_effects=True, vmem_limit_bytes=48 * 2**20
        ),
        cost_estimate=pl.CostEstimate(
            flops=2 * total * d_model * f_dim, bytes_accessed=4 * f_dim * d_model, transcendentals=0
        ),
    )(og, x, rt, ids, hid, w)
    return (grads[None], hidden[None, None], router.T[None])


def solution(mesh):
    placed = (
        P("section", "expert", None),
        P("section", "expert", None),
        P("section", None, None),
        P("section", "expert", None),
        P("section", "expert", None, None),
        P("section", "expert", None, None),
    )
    return jax.shard_map(
        functools.partial(shards, mesh.shape["section"], mesh.shape["expert"]),
        mesh=mesh,
        in_specs=placed,
        out_specs=(
            P("section", "expert", None),
            P("section", "expert", None, None),
            P("section", "expert", None),
        ),
        check_vma=False,
    )
```

```python
import functools

import jax
import jax.numpy as jnp
from jax import lax
from jax.experimental import pallas as pl
from jax.experimental.pallas import tpu as pltpu
from jax.sharding import PartitionSpec as P

MESH = pl.DeviceIdType.MESH
NT = (((1,), (1,)), ((), ()))
TN = (((0,), (0,)), ((), ()))
NN = (((1,), (0,)), ((), ()))
LANES = 128
ROWS_A = 4
CHUNKS = 2
A_UP, A_DOWN, B_NEXT, B_PREV, SIB = range(5)


def dot(lhs, rhs, dims):
    return lax.dot_general(lhs, rhs, dims, preferred_element_type=jnp.float32)


def kernel(
    sections, n, og, x, rt, ids, hid, w, out_g, out_h, out_r,
    xg, xs, meta, dgb, ogn, rtn, lgn, xv, rtv, idv, hv, wv,
    gt, grow, hvt, sel, hs, u, v, dgo, dg2, lg,
    blk_recv, blk_send, meta_recv, meta_send, slab_recv, slab_send,
    dg_recv, dg_send, sec_recv, sec_send, loc,
):
    tokens, d_model = og.shape
    topk = ids.shape[0]
    experts = rt.shape[0]
    slots, f_dim = hid.shape
    cap = slots // n
    feats = out_r.shape[1]
    per_tile = LANES // tokens
    tiles = n // per_tile
    nb = n // (2 * ROWS_A)
    tiles_per_group = tiles // ROWS_A
    rows = tokens // CHUNKS

    me = lax.axis_index("expert")
    sec = lax.axis_index("section")
    c = lax.rem(me, 2)
    b = lax.rem(me // 2, nb)
    a = me // (2 * nb)
    sib = me + 1 - 2 * c
    prev = lax.rem(sec + sections - 1, sections)
    nxt = lax.rem(sec + 1, sections)
    tile = me // per_tile
    offset = lax.rem(me, per_tile) * tokens

    local = [
        pltpu.make_async_copy(x, xv, loc.at[0]),
        pltpu.make_async_copy(rt, rtv, loc.at[1]),
        pltpu.make_async_copy(ids, idv, loc.at[2]),
        pltpu.make_async_copy(og, xg.at[me], loc.at[3]),
        pltpu.make_async_copy(w, wv, loc.at[4]),
        pltpu.make_async_copy(hid, hv, loc.at[5]),
    ]
    for copy in local:
        copy.start()

    barrier = pltpu.get_barrier_semaphore()

    def greet(d, carry):
        pl.semaphore_signal(
            barrier, inc=1, device_id={"expert": lax.rem(me + d, n)}, device_id_type=MESH
        )
        return carry

    lax.fori_loop(1, n, greet, 0)
    near = (prev,) if sections == 2 else (prev, nxt)
    for other in near:
        pl.semaphore_signal(barrier, inc=1, device_id={"section": other}, device_id_type=MESH)
    pl.semaphore_wait(barrier, n - 1 + len(near))

    def block_copy(idx, q, target, way, own=False):
        part = pl.ds(q * rows, rows)
        return pltpu.make_async_remote_copy(
            src_ref=og.at[part] if own else xg.at[idx, part],
            dst_ref=xg.at[idx, part],
            send_sem=blk_send.at[idx, q, way],
            recv_sem=blk_recv.at[idx, q],
            device_id={"expert": target},
            device_id_type=MESH,
        )

    def column_sends(g, q, do, own=False):
        idx = (g * nb + b) * 2 + c

        @pl.when(jnp.logical_and(g <= a, a < ROWS_A - 1))
        def _():
            do(block_copy(idx, q, me + 2 * nb, A_UP, own))

        @pl.when(jnp.logical_and(g >= a, a > 0))
        def _():
            do(block_copy(idx, q, me - 2 * nb, A_DOWN, own))

        @pl.when(b < nb - 1)
        def _():
            do(block_copy(idx, q, me + 2, B_NEXT, own))

        @pl.when(b > 0)
        def _():
            do(block_copy(idx, q, me - 2, B_PREV, own))

        do(block_copy(idx, q, sib, SIB, own))

    def cross_sends(g, b2, q, do):
        idx = (g * nb + b2) * 2 + c
        if nb > 2:
            @pl.when(jnp.logical_and(b2 < b, b < nb - 1))
            def _():
                do(block_copy(idx, q, me + 2, B_NEXT))

            @pl.when(jnp.logical_and(b2 > b, b > 0))
            def _():
                do(block_copy(idx, q, me - 2, B_PREV))

        do(block_copy(idx, q, sib, SIB))

    def section_copy(i, src, dst):
        return pltpu.make_async_remote_copy(
            src_ref=src, dst_ref=dst, send_sem=sec_send.at[i], recv_sem=sec_recv.at[i],
            device_id={"section": prev}, device_id_type=MESH,
        )

    grads_over = section_copy(0, og, ogn)
    router_over = section_copy(1, rt, rtn)
    logit_over = section_copy(2, lg.at[tile], lgn)

    def slab_copy(peer):
        lane = pl.multiple_of((peer * feats) // LANES * LANES, LANES)
        return pltpu.make_async_remote_copy(
            src_ref=x.at[:, pl.ds(lane, LANES)], dst_ref=xs.at[me],
            send_sem=slab_send.at[peer], recv_sem=slab_recv.at[me],
            device_id={"expert": peer}, device_id_type=MESH,
        )

    def meta_copy(peer):
        return pltpu.make_async_remote_copy(
            src_ref=meta.at[me], dst_ref=meta.at[me],
            send_sem=meta_send.at[peer], recv_sem=meta_recv.at[me],
            device_id={"expert": peer}, device_id_type=MESH,
        )

    def dg_copy(peer):
        return pltpu.make_async_remote_copy(
            src_ref=dgo, dst_ref=dgb.at[me],
            send_sem=dg_send.at[peer], recv_sem=dg_recv.at[me],
            device_id={"expert": peer}, device_id_type=MESH,
        )

    def await_from(peer, dst, sem):
        pltpu.make_async_remote_copy(
            src_ref=dst, dst_ref=dst, send_sem=sem, recv_sem=sem,
            device_id={"expert": peer}, device_id_type=MESH,
        ).wait_recv()

    def each_peer(fn):
        def step(d, carry):
            fn(lax.rem(me + d, n))
            return carry

        lax.fori_loop(1, n, step, 0)

    start = lambda copy: copy.start()
    finish = lambda copy: copy.wait_send()

    for q in range(CHUNKS):
        column_sends(a, q, start, own=True)

    own_lane = pl.multiple_of((me * feats) // LANES * LANES, LANES)
    own_slab = pltpu.make_async_copy(x.at[:, pl.ds(own_lane, LANES)], xs.at[me], loc.at[6])
    own_slab.start()
    for copy in local[:3]:
        copy.wait()
    logits = dot(rtv[...], xv[...], NT)
    row = lax.broadcasted_iota(jnp.int32, (experts, tokens), 0)
    named = row == idv[0:1, :]
    for k in range(1, topk):
        named = jnp.logical_or(named, row == idv[k : k + 1, :])
    weights = jnp.where(named, jnp.exp(logits), 0.0)
    gates = weights / jnp.sum(weights, axis=0, keepdims=True)
    marked = jnp.where(named, gates, -1.0).astype(jnp.bfloat16)
    token_of = lax.broadcasted_iota(jnp.int32, (tokens, LANES), 0)
    lane_of = lax.broadcasted_iota(jnp.int32, (tokens, LANES), 1)
    place = jnp.where(lane_of == token_of + offset, 1.0, 0.0).astype(jnp.bfloat16)
    meta[me] = dot(marked, place, NN).astype(jnp.bfloat16)
    each_peer(lambda peer: meta_copy(peer).start())
    each_peer(lambda peer: slab_copy(peer).start())
    grads_over.start()
    router_over.start()
    for copy in local[3:]:
        copy.wait()
    hvt[...] = jnp.transpose(hv[...])

    def order(k):
        closest = jnp.minimum(a, ROWS_A - 1 - a)
        d = (k + 1) // 2
        both = jnp.where(lax.rem(k, 2) == 1, a - d, a + d)
        rest = jnp.where(a <= ROWS_A - 1 - a, k, ROWS_A - 1 - k)
        return jnp.where(k <= 2 * closest, both, rest)

    def slots_of_expert():
        each_peer(lambda peer: await_from(peer, meta.at[peer], meta_recv.at[peer]))
        erow = lax.broadcasted_iota(jnp.int32, (experts, LANES), 0)
        t_from = lax.broadcasted_iota(jnp.int32, (LANES, LANES), 0)
        t_to = lax.broadcasted_iota(jnp.int32, (LANES, LANES), 1)
        ahead = jnp.where(
            jnp.logical_and(t_from < t_to, t_from // tokens == t_to // tokens), 1.0, 0.0
        ).astype(jnp.bfloat16)
        lane_block = lax.broadcasted_iota(jnp.int32, (1, LANES), 1) // tokens
        slot_row = lax.broadcasted_iota(jnp.int32, (slots, LANES), 0)
        for j in range(tiles):
            total = meta[j * per_tile].astype(jnp.float32)
            for i in range(1, per_tile):
                total = total + meta[j * per_tile + i].astype(jnp.float32)
            gt[j] = total
            mine = jnp.sum(jnp.where(erow == me, total, 0.0), axis=0, keepdims=True)
            grow[j : j + 1, :] = jnp.maximum(mine, 0.0)
            taken = jnp.where(mine >= 0.0, 1.0, 0.0)
            many = jnp.broadcast_to(taken, (16, LANES)).astype(jnp.bfloat16)
            rank = dot(many, ahead, NN)[0:1, :].astype(jnp.int32)
            slot = (lane_block + j * per_tile) * cap + rank
            slot = jnp.where(mine >= 0.0, slot, -1)
            hot = jnp.where(slot_row == slot, 1.0, 0.0).astype(jnp.bfloat16)
            sel[:, j * LANES : (j + 1) * LANES] = hot
            hs[j] = dot(hvt[...], hot, NN)

    def products(g):
        for i in range(tiles_per_group):
            t = g * tiles_per_group + i
            u[t] = dot(
                wv[...], xg[pl.ds(t * per_tile, per_tile)].reshape(LANES, d_model), NT
            )

    def gradients(g):
        for i in range(tiles_per_group):
            t = g * tiles_per_group + i
            lanes = pl.ds(pl.multiple_of(t * LANES, LANES), LANES)
            dgo[pl.ds(t, 1), :] = jnp.sum(u[t] * hs[t], axis=0, keepdims=True)
            v[:, lanes] = (u[t] * grow[pl.ds(t, 1), :]).astype(jnp.bfloat16)

    def step(k, carry):
        for q in range(CHUNKS):
            for g, there in ((a - k - 1, a - k - 1 >= 0), (a + k + 1, a + k + 1 < ROWS_A)):
                @pl.when(there)
                def _():
                    block_copy((g * nb + b) * 2 + c, q, sib, SIB).wait_recv()
                    column_sends(g, q, start)

        @pl.when(k < ROWS_A)
        def _():
            g = order(k)
            for j in range(1, nb):
                b2 = lax.rem(b + j, nb)
                for q in range(CHUNKS):
                    block_copy((g * nb + b2) * 2 + c, q, sib, SIB).wait_recv()
                    cross_sends(g, b2, q, start)

        @pl.when(k == 2)
        def _():
            slots_of_expert()

        @pl.when(k > 0)
        def _():
            g = order(k - 1)
            for b2 in range(nb):
                for q in range(CHUNKS):
                    block_copy((g * nb + b2) * 2 + 1 - c, q, sib, SIB).wait_recv()
            products(g)

        @pl.when(k == 2)
        def _():
            gradients(order(0))

        @pl.when(k >= 2)
        def _():
            gradients(order(k - 1))

        return carry

    lax.fori_loop(0, ROWS_A + 1, step, 0)

    each_peer(lambda peer: dg_copy(peer).start())

    out_h[...] = dot(sel[...], v[...], NT).astype(jnp.bfloat16)

    for q in range(CHUNKS):
        column_sends(a, q, finish, own=True)

    def drain(k, carry):
        g = order(k)

        @pl.when(k > 0)
        def _():
            for q in range(CHUNKS):
                column_sends(g, q, finish)

        for j in range(1, nb):
            for q in range(CHUNKS):
                cross_sends(g, lax.rem(b + j, nb), q, finish)
        return carry

    lax.fori_loop(0, ROWS_A, drain, 0)

    def sent(peer):
        meta_copy(peer).wait_send()
        slab_copy(peer).wait_send()

    each_peer(sent)
    grads_over.wait_send()
    router_over.wait_send()

    own_slab.wait()
    each_peer(lambda peer: await_from(peer, xs.at[peer], slab_recv.at[peer]))
    grads_over.wait_recv()
    router_over.wait_recv()

    for j in range(tiles):
        dg2[j, pl.ds(me, 1), :] = dgo[j : j + 1, :]

    def take(peer):
        await_from(peer, dgb.at[peer], dg_recv.at[peer])
        for j in range(tiles):
            dg2[j, pl.ds(peer, 1), :] = dgb[peer, j : j + 1, :]

    each_peer(take)
    for j in range(tiles):
        g = jnp.maximum(gt[j], 0.0)
        d = dg2[j]
        lg[j] = (g * (d - jnp.sum(g * d, axis=0, keepdims=True))).astype(jnp.bfloat16)
    logit_over.start()

    lg_all = jnp.concatenate([lg[j] for j in range(tiles)], axis=1)
    part = dot(lg_all, xs[...].reshape(n * tokens, LANES), NN)
    if feats < LANES:
        shift = lax.rem(LANES - lax.rem(me * feats, LANES), LANES)
        part = pltpu.roll(part, shift, 1)[:, :feats]
    out_r[...] = part

    logit_over.wait_recv()
    mine = dot(place, lgn[...], NT).astype(jnp.bfloat16)
    out_g[...] = (ogn[...].astype(jnp.float32) + dot(mine, rtn[...], NN)).astype(jnp.bfloat16)
    each_peer(lambda peer: dg_copy(peer).wait_send())
    logit_over.wait_send()


def write_out(grads, hidden, router, out_g, out_h, out_r, sem):
    copies = [
        pltpu.make_async_copy(grads, out_g, sem.at[0]),
        pltpu.make_async_copy(hidden, out_h, sem.at[1]),
        pltpu.make_async_copy(router, out_r, sem.at[2]),
    ]
    for copy in copies:
        copy.start()
    for copy in copies:
        copy.wait()


def shards(sections, n, out_grad, layer_input, router_weight, expert_ids, hidden_act, down_weight):
    og, x, hid, w = out_grad[0], layer_input[0], hidden_act[0, 0], down_weight[0, 0]
    rt, ids = router_weight[0].T, expert_ids[0].T
    tokens, d_model = og.shape
    experts, topk = rt.shape[0], ids.shape[0]
    slots, f_dim = hid.shape
    feats = d_model // n
    total = n * tokens
    tiles = total // LANES
    bf16, f32 = jnp.bfloat16, jnp.float32
    dma = pltpu.SemaphoreType.DMA
    hbm = pl.BlockSpec(memory_space=pltpu.HBM)
    vmem = pl.BlockSpec(memory_space=pltpu.VMEM)
    results = (
        jax.ShapeDtypeStruct((tokens, d_model), bf16),
        jax.ShapeDtypeStruct((slots, f_dim), bf16),
        jax.ShapeDtypeStruct((experts, feats), f32),
    )
    held = pl.pallas_call(
        functools.partial(kernel, sections, n),
        out_shape=results,
        in_specs=[hbm] * 6,
        out_specs=(vmem,) * 3,
        scratch_shapes=[
            pltpu.VMEM((n, tokens, d_model), bf16),
            pltpu.VMEM((n, tokens, LANES), bf16),
            pltpu.VMEM((n, experts, LANES), bf16),
            pltpu.VMEM((n, tiles, LANES), f32),
            pltpu.VMEM((tokens, d_model), bf16),
            pltpu.VMEM((experts, d_model), bf16),
            pltpu.VMEM((experts, LANES), bf16),
            pltpu.VMEM((tokens, d_model), bf16),
            pltpu.VMEM((experts, d_model), bf16),
            pltpu.VMEM((topk, tokens), jnp.int32),
            pltpu.VMEM((slots, f_dim), bf16),
            pltpu.VMEM((f_dim, d_model), bf16),
            pltpu.VMEM((tiles, experts, LANES), f32),
            pltpu.VMEM((tiles, LANES), f32),
            pltpu.VMEM((f_dim, slots), bf16),
            pltpu.VMEM((slots, total), bf16),
            pltpu.VMEM((tiles, f_dim, LANES), f32),
            pltpu.VMEM((tiles, f_dim, LANES), f32),
            pltpu.VMEM((f_dim, total), bf16),
            pltpu.VMEM((tiles, LANES), f32),
            pltpu.VMEM((tiles, experts, LANES), f32),
            pltpu.VMEM((tiles, experts, LANES), bf16),
            dma((n, CHUNKS)),
            dma((n, CHUNKS, 5)),
            dma((n,)),
            dma((n,)),
            dma((n,)),
            dma((n,)),
            dma((n,)),
            dma((n,)),
            dma((3,)),
            dma((3,)),
            dma((7,)),
        ],
        compiler_params=pltpu.CompilerParams(
            collective_id=0, has_side_effects=True, vmem_limit_bytes=48 * 2**20
        ),
        cost_estimate=pl.CostEstimate(
            flops=2 * total * d_model * f_dim, bytes_accessed=4 * f_dim * d_model, transcendentals=0
        ),
    )(*(pltpu.with_memory_space_constraint(p, pltpu.HBM) for p in (og, x, rt, ids, hid, w)))
    grads, hidden, router = pl.pallas_call(
        write_out,
        out_shape=results,
        in_specs=[vmem] * 3,
        out_specs=(hbm,) * 3,
        scratch_shapes=[dma((3,))],
    )(*held)
    return (grads[None], hidden[None, None], router.T[None])


def solution(mesh):
    placed = (
        P("section", "expert", None),
        P("section", "expert", None),
        P("section", None, None),
        P("section", "expert", None),
        P("section", "expert", None, None),
        P("section", "expert", None, None),
    )
    return jax.shard_map(
        functools.partial(shards, mesh.shape["section"], mesh.shape["expert"]),
        mesh=mesh,
        in_specs=placed,
        out_specs=(
            P("section", "expert", None),
            P("section", "expert", None, None),
            P("section", "expert", None),
        ),
        check_vma=False,
    )
```

```python
import functools

import jax
import jax.numpy as jnp
from jax import lax
from jax.experimental import pallas as pl
from jax.experimental.pallas import tpu as pltpu
from jax.sharding import PartitionSpec as P

MESH = pl.DeviceIdType.MESH
NT = (((1,), (1,)), ((), ()))
TN = (((0,), (0,)), ((), ()))
NN = (((1,), (0,)), ((), ()))
LANES = 128
ROWS_A = 4
CHUNKS = 2
A_UP, A_DOWN, B_NEXT, B_PREV, SIB = range(5)


def dot(lhs, rhs, dims):
    return lax.dot_general(lhs, rhs, dims, preferred_element_type=jnp.float32)


def kernel(
    sections, n, og, x, rt, ids, hid, w, out_g, out_h, out_r,
    xg, xs, meta, dgb, ogn, rtn, lgn, xv, rtv, idv, hv, wv,
    gt, grow, hvt, sel, hs, u, v, dgo, dg2, lg,
    blk_recv, blk_send, meta_recv, meta_send, slab_recv, slab_send,
    dg_recv, dg_send, sec_recv, sec_send, loc,
):
    tokens, d_model = og.shape
    topk = ids.shape[0]
    experts = rt.shape[0]
    slots, f_dim = hid.shape
    cap = slots // n
    feats = out_r.shape[1]
    per_tile = LANES // tokens
    tiles = n // per_tile
    nb = n // (2 * ROWS_A)
    tiles_per_group = tiles // ROWS_A
    rows = tokens // CHUNKS

    me = lax.axis_index("expert")
    sec = lax.axis_index("section")
    c = lax.rem(me, 2)
    b = lax.rem(me // 2, nb)
    a = me // (2 * nb)
    sib = me + 1 - 2 * c
    prev = lax.rem(sec + sections - 1, sections)
    nxt = lax.rem(sec + 1, sections)
    tile = me // per_tile
    offset = lax.rem(me, per_tile) * tokens

    ring = lambda i: jnp.where(i >= n, i - n, i)

    local = [
        pltpu.make_async_copy(x, xv, loc.at[0]),
        pltpu.make_async_copy(rt, rtv, loc.at[1]),
        pltpu.make_async_copy(ids, idv, loc.at[2]),
        pltpu.make_async_copy(og, xg.at[me], loc.at[3]),
        pltpu.make_async_copy(w, wv, loc.at[4]),
        pltpu.make_async_copy(hid, hv, loc.at[5]),
    ]
    for copy in local:
        copy.start()

    barrier = pltpu.get_barrier_semaphore()

    def greet(d, carry):
        pl.semaphore_signal(
            barrier, inc=1, device_id={"expert": ring(me + d)}, device_id_type=MESH
        )
        return carry

    lax.fori_loop(1, n, greet, 0)
    near = (prev,) if sections == 2 else (prev, nxt)
    for other in near:
        pl.semaphore_signal(barrier, inc=1, device_id={"section": other}, device_id_type=MESH)
    pl.semaphore_wait(barrier, n - 1 + len(near))

    def block_copy(idx, q, target, way, own=False):
        part = pl.ds(q * rows, rows)
        return pltpu.make_async_remote_copy(
            src_ref=og.at[part] if own else xg.at[idx, part],
            dst_ref=xg.at[idx, part],
            send_sem=blk_send.at[idx, q, way],
            recv_sem=blk_recv.at[idx, q],
            device_id={"expert": target},
            device_id_type=MESH,
        )

    def at_end(g):
        return jnp.logical_or(g == 0, g == ROWS_A - 1)

    def crossed_early(g, q):
        if nb > 2 or q > 0:
            return jnp.logical_and(g == a, g != a)
        return jnp.logical_and(at_end(g), g != a)

    def column_sends(g, q, do, own=False):
        idx = (g * nb + b) * 2 + c
        crosses = jnp.logical_not(crossed_early(g, q))

        @pl.when(jnp.logical_and(g <= a, a < ROWS_A - 1))
        def _():
            do(block_copy(idx, q, me + 2 * nb, A_UP, own))

        @pl.when(jnp.logical_and(g >= a, a > 0))
        def _():
            do(block_copy(idx, q, me - 2 * nb, A_DOWN, own))

        @pl.when(jnp.logical_and(crosses, b < nb - 1))
        def _():
            do(block_copy(idx, q, me + 2, B_NEXT, own))

        @pl.when(jnp.logical_and(crosses, b > 0))
        def _():
            do(block_copy(idx, q, me - 2, B_PREV, own))

        do(block_copy(idx, q, sib, SIB, own))

    def cross_sends(g, b2, q, do):
        idx = (g * nb + b2) * 2 + c
        if nb > 2:
            @pl.when(jnp.logical_and(b2 < b, b < nb - 1))
            def _():
                do(block_copy(idx, q, me + 2, B_NEXT))

            @pl.when(jnp.logical_and(b2 > b, b > 0))
            def _():
                do(block_copy(idx, q, me - 2, B_PREV))

        elif q == 0:
            @pl.when(jnp.logical_and(at_end(g), jnp.logical_and(g <= a, a < ROWS_A - 1)))
            def _():
                do(block_copy(idx, q, me + 2 * nb, A_UP))

            @pl.when(jnp.logical_and(at_end(g), jnp.logical_and(g >= a, a > 0)))
            def _():
                do(block_copy(idx, q, me - 2 * nb, A_DOWN))

        do(block_copy(idx, q, sib, SIB))

    def section_copy(i, src, dst):
        return pltpu.make_async_remote_copy(
            src_ref=src, dst_ref=dst, send_sem=sec_send.at[i], recv_sem=sec_recv.at[i],
            device_id={"section": prev}, device_id_type=MESH,
        )

    grads_over = section_copy(0, og, ogn)
    router_over = section_copy(1, rt, rtn)
    logit_over = section_copy(2, lg.at[tile], lgn)

    def slab_copy(peer):
        lane = pl.multiple_of((peer * feats) // LANES * LANES, LANES)
        return pltpu.make_async_remote_copy(
            src_ref=x.at[:, pl.ds(lane, LANES)], dst_ref=xs.at[me],
            send_sem=slab_send.at[peer], recv_sem=slab_recv.at[me],
            device_id={"expert": peer}, device_id_type=MESH,
        )

    def meta_copy(peer):
        return pltpu.make_async_remote_copy(
            src_ref=meta.at[me], dst_ref=meta.at[me],
            send_sem=meta_send.at[peer], recv_sem=meta_recv.at[me],
            device_id={"expert": peer}, device_id_type=MESH,
        )

    def dg_copy(peer):
        return pltpu.make_async_remote_copy(
            src_ref=dgo, dst_ref=dgb.at[me],
            send_sem=dg_send.at[peer], recv_sem=dg_recv.at[me],
            device_id={"expert": peer}, device_id_type=MESH,
        )

    def await_from(peer, dst, sem):
        pltpu.make_async_remote_copy(
            src_ref=dst, dst_ref=dst, send_sem=sem, recv_sem=sem,
            device_id={"expert": peer}, device_id_type=MESH,
        ).wait_recv()

    def each_peer(fn):
        def step(d, carry):
            fn(ring(me + d))
            return carry

        lax.fori_loop(1, n, step, 0)

    start = lambda copy: copy.start()
    finish = lambda copy: copy.wait_send()

    for q in range(CHUNKS):
        column_sends(a, q, start, own=True)

    own_lane = pl.multiple_of((me * feats) // LANES * LANES, LANES)
    own_slab = pltpu.make_async_copy(x.at[:, pl.ds(own_lane, LANES)], xs.at[me], loc.at[6])
    own_slab.start()
    for copy in local[:3]:
        copy.wait()
    logits = dot(rtv[...], xv[...], NT)
    row = lax.broadcasted_iota(jnp.int32, (experts, tokens), 0)
    named = row == idv[0:1, :]
    for k in range(1, topk):
        named = jnp.logical_or(named, row == idv[k : k + 1, :])
    weights = jnp.where(named, jnp.exp(logits), 0.0)
    gates = weights / jnp.sum(weights, axis=0, keepdims=True)
    marked = jnp.where(named, gates, -1.0).astype(jnp.bfloat16)
    token_of = lax.broadcasted_iota(jnp.int32, (tokens, LANES), 0)
    lane_of = lax.broadcasted_iota(jnp.int32, (tokens, LANES), 1)
    place = jnp.where(lane_of == token_of + offset, 1.0, 0.0).astype(jnp.bfloat16)
    meta[me] = dot(marked, place, NN).astype(jnp.bfloat16)
    each_peer(lambda peer: meta_copy(peer).start())
    each_peer(lambda peer: slab_copy(peer).start())
    grads_over.start()
    router_over.start()
    for copy in local[3:]:
        copy.wait()
    hvt[...] = jnp.transpose(hv[...])

    def order(k):
        closest = jnp.minimum(a, ROWS_A - 1 - a)
        d = (k + 1) // 2
        both = jnp.where(lax.rem(k, 2) == 1, a - d, a + d)
        rest = jnp.where(a <= ROWS_A - 1 - a, k, ROWS_A - 1 - k)
        return jnp.where(k <= 2 * closest, both, rest)

    def slots_of_expert():
        each_peer(lambda peer: await_from(peer, meta.at[peer], meta_recv.at[peer]))
        erow = lax.broadcasted_iota(jnp.int32, (experts, LANES), 0)
        t_from = lax.broadcasted_iota(jnp.int32, (LANES, LANES), 0)
        t_to = lax.broadcasted_iota(jnp.int32, (LANES, LANES), 1)
        ahead = jnp.where(
            jnp.logical_and(t_from < t_to, t_from // tokens == t_to // tokens), 1.0, 0.0
        ).astype(jnp.bfloat16)
        lane_block = lax.broadcasted_iota(jnp.int32, (1, LANES), 1) // tokens
        slot_row = lax.broadcasted_iota(jnp.int32, (slots, LANES), 0)
        for j in range(tiles):
            total = meta[j * per_tile].astype(jnp.float32)
            for i in range(1, per_tile):
                total = total + meta[j * per_tile + i].astype(jnp.float32)
            gt[j] = total
            mine = jnp.sum(jnp.where(erow == me, total, 0.0), axis=0, keepdims=True)
            grow[j : j + 1, :] = jnp.maximum(mine, 0.0)
            taken = jnp.where(mine >= 0.0, 1.0, 0.0)
            many = jnp.broadcast_to(taken, (16, LANES)).astype(jnp.bfloat16)
            rank = dot(many, ahead, NN)[0:1, :].astype(jnp.int32)
            slot = (lane_block + j * per_tile) * cap + rank
            slot = jnp.where(mine >= 0.0, slot, -1)
            hot = jnp.where(slot_row == slot, 1.0, 0.0).astype(jnp.bfloat16)
            sel[:, j * LANES : (j + 1) * LANES] = hot
            hs[j] = dot(hvt[...], hot, NN)

    def products(g):
        for i in range(tiles_per_group):
            t = g * tiles_per_group + i
            u[t] = dot(
                wv[...], xg[pl.ds(t * per_tile, per_tile)].reshape(LANES, d_model), NT
            )

    def gradients(g):
        for i in range(tiles_per_group):
            t = g * tiles_per_group + i
            lanes = pl.ds(pl.multiple_of(t * LANES, LANES), LANES)
            dgo[pl.ds(t, 1), :] = jnp.sum(u[t] * hs[t], axis=0, keepdims=True)
            v[:, lanes] = (u[t] * grow[pl.ds(t, 1), :]).astype(jnp.bfloat16)

    def from_sibling(g):
        for b2 in range(nb):
            for q in range(CHUNKS):
                block_copy((g * nb + b2) * 2 + 1 - c, q, sib, SIB).wait_recv()
        products(g)

    def sent(peer):
        meta_copy(peer).wait_send()
        slab_copy(peer).wait_send()

    def step(k, carry):
        for q in range(CHUNKS):
            for g, there in ((a - k - 1, a - k - 1 >= 0), (a + k + 1, a + k + 1 < ROWS_A)):
                @pl.when(there)
                def _():
                    block_copy((g * nb + b) * 2 + c, q, sib, SIB).wait_recv()
                    column_sends(g, q, start)

        if nb == 2:
            for g, there in ((a - k - 1, a - k - 1 >= 0), (a + k + 1, a + k + 1 < ROWS_A)):
                @pl.when(jnp.logical_and(there, at_end(g)))
                def _():
                    block_copy((g * nb + 1 - b) * 2 + c, 0, sib, SIB).wait_recv()
                    cross_sends(g, 1 - b, 0, start)

        @pl.when(jnp.logical_and(k > 0, k < ROWS_A))
        def _():
            from_sibling(order(k - 1))

        @pl.when(k == 2)
        def _():
            slots_of_expert()
            gradients(order(0))

        @pl.when(jnp.logical_and(k >= 2, k < ROWS_A))
        def _():
            gradients(order(k - 1))

        @pl.when(k == ROWS_A - 1)
        def _():
            for q in range(CHUNKS):
                column_sends(a, q, finish, own=True)
            each_peer(sent)

        g = order(k)
        for j in range(1, nb):
            b2 = lax.rem(b + j, nb)
            for q in range(CHUNKS):
                @pl.when(jnp.logical_not(crossed_early(g, q)))
                def _():
                    block_copy((g * nb + b2) * 2 + c, q, sib, SIB).wait_recv()
                    cross_sends(g, b2, q, start)

        return carry

    lax.fori_loop(0, ROWS_A, step, 0)
    from_sibling(order(ROWS_A - 1))
    gradients(order(ROWS_A - 1))

    each_peer(lambda peer: dg_copy(peer).start())

    out_h[...] = dot(sel[...], v[...], NT).astype(jnp.bfloat16)

    own_slab.wait()
    each_peer(lambda peer: await_from(peer, xs.at[peer], slab_recv.at[peer]))
    grads_over.wait_recv()
    router_over.wait_recv()

    for j in range(tiles):
        dg2[j, pl.ds(me, 1), :] = dgo[j : j + 1, :]

    def take(peer):
        await_from(peer, dgb.at[peer], dg_recv.at[peer])
        for j in range(tiles):
            dg2[j, pl.ds(peer, 1), :] = dgb[peer, j : j + 1, :]

    each_peer(take)
    for j in range(tiles):
        g = jnp.maximum(gt[j], 0.0)
        d = dg2[j]
        lg[j] = (g * (d - jnp.sum(g * d, axis=0, keepdims=True))).astype(jnp.bfloat16)
    logit_over.start()

    lg_all = jnp.concatenate([lg[j] for j in range(tiles)], axis=1)
    part = dot(lg_all, xs[...].reshape(n * tokens, LANES), NN)
    if feats < LANES:
        shift = lax.rem(LANES - lax.rem(me * feats, LANES), LANES)
        part = pltpu.roll(part, shift, 1)[:, :feats]
    out_r[...] = part

    def drain(k, carry):
        g = order(k)

        @pl.when(k > 0)
        def _():
            for q in range(CHUNKS):
                column_sends(g, q, finish)

        for j in range(1, nb):
            for q in range(CHUNKS):
                cross_sends(g, lax.rem(b + j, nb), q, finish)
        return carry

    lax.fori_loop(0, ROWS_A, drain, 0)
    grads_over.wait_send()
    router_over.wait_send()

    logit_over.wait_recv()
    mine = dot(place, lgn[...], NT).astype(jnp.bfloat16)
    out_g[...] = (ogn[...].astype(jnp.float32) + dot(mine, rtn[...], NN)).astype(jnp.bfloat16)
    each_peer(lambda peer: dg_copy(peer).wait_send())
    logit_over.wait_send()


def write_out(grads, hidden, router, out_g, out_h, out_r, sem):
    copies = [
        pltpu.make_async_copy(grads, out_g, sem.at[0]),
        pltpu.make_async_copy(hidden, out_h, sem.at[1]),
        pltpu.make_async_copy(router, out_r, sem.at[2]),
    ]
    for copy in copies:
        copy.start()
    for copy in copies:
        copy.wait()


def shards(sections, n, out_grad, layer_input, router_weight, expert_ids, hidden_act, down_weight):
    og, x, hid, w = out_grad[0], layer_input[0], hidden_act[0, 0], down_weight[0, 0]
    rt, ids = router_weight[0].T, expert_ids[0].T
    tokens, d_model = og.shape
    experts, topk = rt.shape[0], ids.shape[0]
    slots, f_dim = hid.shape
    feats = d_model // n
    total = n * tokens
    tiles = total // LANES
    bf16, f32 = jnp.bfloat16, jnp.float32
    dma = pltpu.SemaphoreType.DMA
    hbm = pl.BlockSpec(memory_space=pltpu.HBM)
    vmem = pl.BlockSpec(memory_space=pltpu.VMEM)
    results = (
        jax.ShapeDtypeStruct((tokens, d_model), bf16),
        jax.ShapeDtypeStruct((slots, f_dim), bf16),
        jax.ShapeDtypeStruct((experts, feats), f32),
    )
    held = pl.pallas_call(
        functools.partial(kernel, sections, n),
        out_shape=tuple(pltpu.VMEM(r.shape, r.dtype) for r in results),
        in_specs=[hbm] * 6,
        out_specs=(vmem,) * 3,
        scratch_shapes=[
            pltpu.VMEM((n, tokens, d_model), bf16),
            pltpu.VMEM((n, tokens, LANES), bf16),
            pltpu.VMEM((n, experts, LANES), bf16),
            pltpu.VMEM((n, tiles, LANES), f32),
            pltpu.VMEM((tokens, d_model), bf16),
            pltpu.VMEM((experts, d_model), bf16),
            pltpu.VMEM((experts, LANES), bf16),
            pltpu.VMEM((tokens, d_model), bf16),
            pltpu.VMEM((experts, d_model), bf16),
            pltpu.VMEM((topk, tokens), jnp.int32),
            pltpu.VMEM((slots, f_dim), bf16),
            pltpu.VMEM((f_dim, d_model), bf16),
            pltpu.VMEM((tiles, experts, LANES), f32),
            pltpu.VMEM((tiles, LANES), f32),
            pltpu.VMEM((f_dim, slots), bf16),
            pltpu.VMEM((slots, total), bf16),
            pltpu.VMEM((tiles, f_dim, LANES), f32),
            pltpu.VMEM((tiles, f_dim, LANES), f32),
            pltpu.VMEM((f_dim, total), bf16),
            pltpu.VMEM((tiles, LANES), f32),
            pltpu.VMEM((tiles, experts, LANES), f32),
            pltpu.VMEM((tiles, experts, LANES), bf16),
            dma((n, CHUNKS)),
            dma((n, CHUNKS, 5)),
            dma((n,)),
            dma((n,)),
            dma((n,)),
            dma((n,)),
            dma((n,)),
            dma((n,)),
            dma((3,)),
            dma((3,)),
            dma((7,)),
        ],
        compiler_params=pltpu.CompilerParams(
            collective_id=0, has_side_effects=True, vmem_limit_bytes=48 * 2**20
        ),
        cost_estimate=pl.CostEstimate(
            flops=2 * total * d_model * f_dim, bytes_accessed=4 * f_dim * d_model, transcendentals=0
        ),
    )(*(pltpu.with_memory_space_constraint(p, pltpu.HBM) for p in (og, x, rt, ids, hid, w)))
    grads, hidden, router = pl.pallas_call(
        write_out,
        out_shape=results,
        in_specs=[vmem] * 3,
        out_specs=(hbm,) * 3,
        scratch_shapes=[dma((3,))],
    )(*held)
    return (grads[None], hidden[None, None], router.T[None])


def solution(mesh):
    placed = (
        P("section", "expert", None),
        P("section", "expert", None),
        P("section", None, None),
        P("section", "expert", None),
        P("section", "expert", None, None),
        P("section", "expert", None, None),
    )
    return jax.shard_map(
        functools.partial(shards, mesh.shape["section"], mesh.shape["expert"]),
        mesh=mesh,
        in_specs=placed,
        out_specs=(
            P("section", "expert", None),
            P("section", "expert", None, None),
            P("section", "expert", None),
        ),
        check_vma=False,
    )
```

```python
import functools

import jax
import jax.numpy as jnp
from jax import lax
from jax.experimental import pallas as pl
from jax.experimental.pallas import tpu as pltpu
from jax.sharding import PartitionSpec as P

MESH = pl.DeviceIdType.MESH
NT = (((1,), (1,)), ((), ()))
TN = (((0,), (0,)), ((), ()))
NN = (((1,), (0,)), ((), ()))
LANES = 128
ROWS_A = 4
CHUNKS = 1
A_UP, A_DOWN, B_NEXT, B_PREV, SIB = range(5)


def dot(lhs, rhs, dims):
    return lax.dot_general(lhs, rhs, dims, preferred_element_type=jnp.float32)


def kernel(
    sections, n, og, x, rt, ids, hid, w, out_g, out_h, out_r,
    xg, xs, stage, dgb, ogn, rtn, lgn, xv, rtv, idv, hv, wv,
    gt, grow, hvt, sel, hs, u, v, dgo, dg2, lg, outv, hgv, rgv,
    blk_recv, blk_send, sib_recv, peer_recv, peer_send, sec_recv, sec_send, loc,
):
    tokens, d_model = og.shape
    topk = ids.shape[0]
    experts = rt.shape[0]
    slots, f_dim = hid.shape
    cap = slots // n
    feats = out_r.shape[1]
    per_tile = LANES // tokens
    tiles = n // per_tile
    nb = n // (2 * ROWS_A)
    tiles_per_group = tiles // ROWS_A
    rows = tokens // CHUNKS

    me = lax.axis_index("expert")
    sec = lax.axis_index("section")
    c = lax.rem(me, 2)
    b = lax.rem(me // 2, nb)
    a = me // (2 * nb)
    sib = me + 1 - 2 * c
    prev = lax.rem(sec + sections - 1, sections)
    nxt = lax.rem(sec + 1, sections)
    tile = me // per_tile
    offset = lax.rem(me, per_tile) * tokens

    ring = lambda i: jnp.where(i >= n, i - n, i)

    local = [
        pltpu.make_async_copy(x, xv, loc.at[0]),
        pltpu.make_async_copy(rt, rtv, loc.at[1]),
        pltpu.make_async_copy(ids, idv, loc.at[2]),
        pltpu.make_async_copy(og, xg.at[me], loc.at[3]),
        pltpu.make_async_copy(w, wv, loc.at[4]),
        pltpu.make_async_copy(hid, hv, loc.at[5]),
    ]
    for copy in local:
        copy.start()

    barrier = pltpu.get_barrier_semaphore()

    def greet(d, carry):
        pl.semaphore_signal(
            barrier, inc=1, device_id={"expert": ring(me + d)}, device_id_type=MESH
        )
        return carry

    lax.fori_loop(1, n, greet, 0)
    near = (prev,) if sections == 2 else (prev, nxt)
    for other in near:
        pl.semaphore_signal(barrier, inc=1, device_id={"section": other}, device_id_type=MESH)
    pl.semaphore_wait(barrier, n - 1 + len(near))

    start = lambda copy: copy.start()
    finish = lambda copy: copy.wait_send()

    def whole(ref, sem):
        return pltpu.make_async_remote_copy(
            src_ref=ref, dst_ref=ref, send_sem=sem, recv_sem=sem,
            device_id={"expert": sib}, device_id_type=MESH,
        )

    def block_copy(idx, q, target, way, own=False):
        part = pl.ds(q * rows, rows)
        return pltpu.make_async_remote_copy(
            src_ref=og.at[part] if own else xg.at[idx, part],
            dst_ref=xg.at[idx, part],
            send_sem=peer_send.at[2] if way == SIB else blk_send.at[idx, q, way],
            recv_sem=sib_recv.at[idx // (2 * nb)] if way == SIB else blk_recv.at[idx, q],
            device_id={"expert": target},
            device_id_type=MESH,
        )

    def column_sends(g, q, do, own=False):
        idx = (g * nb + b) * 2 + c

        @pl.when(jnp.logical_and(g <= a, a < ROWS_A - 1))
        def _():
            do(block_copy(idx, q, me + 2 * nb, A_UP, own))

        @pl.when(jnp.logical_and(g >= a, a > 0))
        def _():
            do(block_copy(idx, q, me - 2 * nb, A_DOWN, own))

        @pl.when(b < nb - 1)
        def _():
            do(block_copy(idx, q, me + 2, B_NEXT, own))

        @pl.when(b > 0)
        def _():
            do(block_copy(idx, q, me - 2, B_PREV, own))

        if do is start:
            do(block_copy(idx, q, sib, SIB, own))

    def cross_sends(g, b2, q, do):
        idx = (g * nb + b2) * 2 + c
        if nb > 2:
            @pl.when(jnp.logical_and(b2 < b, b < nb - 1))
            def _():
                do(block_copy(idx, q, me + 2, B_NEXT))

            @pl.when(jnp.logical_and(b2 > b, b > 0))
            def _():
                do(block_copy(idx, q, me - 2, B_PREV))

        if do is start:
            do(block_copy(idx, q, sib, SIB))

    def section_copy(i, src, dst):
        return pltpu.make_async_remote_copy(
            src_ref=src, dst_ref=dst, send_sem=sec_send.at[i], recv_sem=sec_recv.at[i],
            device_id={"section": prev}, device_id_type=MESH,
        )

    grads_over = section_copy(0, og, ogn)
    router_over = section_copy(1, rt, rtn)
    logit_over = section_copy(2, lg.at[tile], lgn)

    def mixed_copy(peer):
        return pltpu.make_async_remote_copy(
            src_ref=stage.at[peer], dst_ref=xs.at[me],
            send_sem=peer_send.at[0], recv_sem=peer_recv.at[0],
            device_id={"expert": peer}, device_id_type=MESH,
        )

    def dg_copy(peer):
        return pltpu.make_async_remote_copy(
            src_ref=dgo, dst_ref=dgb.at[me],
            send_sem=peer_send.at[1], recv_sem=peer_recv.at[1],
            device_id={"expert": peer}, device_id_type=MESH,
        )

    def each_peer(fn):
        def step(d, carry):
            fn(ring(me + d))
            return carry

        lax.fori_loop(1, n, step, 0)


    for q in range(CHUNKS):
        column_sends(a, q, start, own=True)

    for copy in local[:3]:
        copy.wait()
    logits = dot(rtv[...], xv[...], NT)
    row = lax.broadcasted_iota(jnp.int32, (experts, tokens), 0)
    named = row == idv[0:1, :]
    for k in range(1, topk):
        named = jnp.logical_or(named, row == idv[k : k + 1, :])
    weights = jnp.where(named, jnp.exp(logits), 0.0)
    gates = weights / jnp.sum(weights, axis=0, keepdims=True)
    marked = jnp.where(named, gates, -1.0).astype(jnp.bfloat16)
    token_of = lax.broadcasted_iota(jnp.int32, (tokens, LANES), 0)
    lane_of = lax.broadcasted_iota(jnp.int32, (tokens, LANES), 1)
    place = jnp.where(lane_of == token_of + offset, 1.0, 0.0).astype(jnp.bfloat16)
    mark = dot(marked, place, NN).astype(jnp.bfloat16)
    for peer in range(n):
        lane = peer * feats // LANES * LANES
        stage[peer, :tokens, :] = xv[:, lane : lane + LANES]
        stage[peer, tokens:, :] = mark
    xs[me] = stage[me]
    each_peer(lambda peer: mixed_copy(peer).start())
    grads_over.start()
    router_over.start()
    for copy in local[3:]:
        copy.wait()
    hvt[...] = jnp.transpose(hv[...])

    def order(k):
        closest = jnp.minimum(a, ROWS_A - 1 - a)
        d = (k + 1) // 2
        both = jnp.where(lax.rem(k, 2) == 1, a - d, a + d)
        rest = jnp.where(a <= ROWS_A - 1 - a, k, ROWS_A - 1 - k)
        return jnp.where(k <= 2 * closest, both, rest)

    def slots_of_expert():
        whole(xs.at[pl.ds(0, n - 1)], peer_recv.at[0]).wait_recv()
        erow = lax.broadcasted_iota(jnp.int32, (experts, LANES), 0)
        t_from = lax.broadcasted_iota(jnp.int32, (LANES, LANES), 0)
        t_to = lax.broadcasted_iota(jnp.int32, (LANES, LANES), 1)
        ahead = jnp.where(
            jnp.logical_and(t_from < t_to, t_from // tokens == t_to // tokens), 1.0, 0.0
        ).astype(jnp.bfloat16)
        lane_block = lax.broadcasted_iota(jnp.int32, (1, LANES), 1) // tokens
        slot_row = lax.broadcasted_iota(jnp.int32, (slots, LANES), 0)
        for j in range(tiles):
            total = xs[j * per_tile, tokens:, :].astype(jnp.float32)
            for i in range(1, per_tile):
                total = total + xs[j * per_tile + i, tokens:, :].astype(jnp.float32)
            gt[j] = total
            mine = jnp.sum(jnp.where(erow == me, total, 0.0), axis=0, keepdims=True)
            grow[j : j + 1, :] = jnp.maximum(mine, 0.0)
            taken = jnp.where(mine >= 0.0, 1.0, 0.0)
            many = jnp.broadcast_to(taken, (16, LANES)).astype(jnp.bfloat16)
            rank = dot(many, ahead, NN)[0:1, :].astype(jnp.int32)
            slot = (lane_block + j * per_tile) * cap + rank
            slot = jnp.where(mine >= 0.0, slot, -1)
            hot = jnp.where(slot_row == slot, 1.0, 0.0).astype(jnp.bfloat16)
            sel[:, j * LANES : (j + 1) * LANES] = hot
            hs[j] = dot(hvt[...], hot, NN)

    def products(g):
        for i in range(tiles_per_group):
            t = g * tiles_per_group + i
            u[t] = dot(
                wv[...], xg[pl.ds(t * per_tile, per_tile)].reshape(LANES, d_model), NT
            )

    def gradients(g):
        for i in range(tiles_per_group):
            t = g * tiles_per_group + i
            lanes = pl.ds(pl.multiple_of(t * LANES, LANES), LANES)
            dgo[pl.ds(t, 1), :] = jnp.sum(u[t] * hs[t], axis=0, keepdims=True)
            v[:, lanes] = (u[t] * grow[pl.ds(t, 1), :]).astype(jnp.bfloat16)

    def step(k, carry):
        for q in range(CHUNKS):
            for g, there in ((a - k - 1, a - k - 1 >= 0), (a + k + 1, a + k + 1 < ROWS_A)):
                @pl.when(there)
                def _():
                    block_copy((g * nb + b) * 2 + c, q, sib, A_UP).wait_recv()
                    column_sends(g, q, start)

        @pl.when(k < ROWS_A)
        def _():
            g = order(k)
            for j in range(1, nb):
                b2 = lax.rem(b + j, nb)
                for q in range(CHUNKS):
                    block_copy((g * nb + b2) * 2 + c, q, sib, A_UP).wait_recv()
                    cross_sends(g, b2, q, start)

        @pl.when(k == 2)
        def _():
            slots_of_expert()

        @pl.when(k > 0)
        def _():
            g = order(k - 1)
            whole(xg.at[pl.ds(g * 2 * nb, nb)], sib_recv.at[g]).wait_recv()
            products(g)

        @pl.when(k == 2)
        def _():
            gradients(order(0))

        @pl.when(k >= 2)
        def _():
            gradients(order(k - 1))

        return carry

    lax.fori_loop(0, ROWS_A + 1, step, 0)

    each_peer(lambda peer: dg_copy(peer).start())

    hgv[...] = dot(sel[...], v[...], NT).astype(jnp.bfloat16)
    hidden_out = pltpu.make_async_copy(hgv, out_h, loc.at[6])
    hidden_out.start()
    grads_over.wait_recv()
    router_over.wait_recv()
    dgb[me] = dgo[...]
    whole(dgb.at[pl.ds(0, n - 1)], peer_recv.at[1]).wait_recv()
    for peer in range(n):
        for j in range(tiles):
            dg2[j, peer : peer + 1, :] = dgb[peer, j : j + 1, :]
    for j in range(tiles):
        g = jnp.maximum(gt[j], 0.0)
        d = dg2[j]
        lg[j] = (g * (d - jnp.sum(g * d, axis=0, keepdims=True))).astype(jnp.bfloat16)
    logit_over.start()

    lg_all = jnp.concatenate([lg[j] for j in range(tiles)], axis=1)
    part = dot(lg_all, xs[:, :tokens, :].reshape(n * tokens, LANES), NN)
    if feats < LANES:
        shift = lax.rem(LANES - lax.rem(me * feats, LANES), LANES)
        part = pltpu.roll(part, shift, 1)[:, :feats]
    rgv[...] = part
    router_out = pltpu.make_async_copy(rgv, out_r, loc.at[7])
    router_out.start()

    for q in range(CHUNKS):
        column_sends(a, q, finish, own=True)

    def drain(k, carry):
        g = order(k)

        @pl.when(k > 0)
        def _():
            for q in range(CHUNKS):
                column_sends(g, q, finish)

        if nb > 2:
            for j in range(1, nb):
                for q in range(CHUNKS):
                    cross_sends(g, lax.rem(b + j, nb), q, finish)
        return carry

    lax.fori_loop(0, ROWS_A, drain, 0)
    whole(xg.at[pl.ds(0, n // 2)], peer_send.at[2]).wait_send()
    whole(stage.at[pl.ds(0, n - 1)], peer_send.at[0]).wait_send()
    whole(dgb.at[pl.ds(0, n - 1)], peer_send.at[1]).wait_send()
    grads_over.wait_send()
    router_over.wait_send()

    logit_over.wait_recv()
    mine = dot(place, lgn[...], NT).astype(jnp.bfloat16)
    outv[...] = (ogn[...].astype(jnp.float32) + dot(mine, rtn[...], NN)).astype(jnp.bfloat16)
    grads_out = pltpu.make_async_copy(outv, out_g, loc.at[8])
    grads_out.start()
    logit_over.wait_send()
    hidden_out.wait()
    router_out.wait()
    grads_out.wait()


def shards(sections, n, out_grad, layer_input, router_weight, expert_ids, hidden_act, down_weight):
    og, x, hid, w = out_grad[0], layer_input[0], hidden_act[0, 0], down_weight[0, 0]
    rt, ids = router_weight[0].T, expert_ids[0].T
    tokens, d_model = og.shape
    experts, topk = rt.shape[0], ids.shape[0]
    slots, f_dim = hid.shape
    feats = d_model // n
    total = n * tokens
    tiles = total // LANES
    bf16, f32 = jnp.bfloat16, jnp.float32
    dma = pltpu.SemaphoreType.DMA
    hbm = pl.BlockSpec(memory_space=pltpu.HBM)
    results = (
        jax.ShapeDtypeStruct((tokens, d_model), bf16),
        jax.ShapeDtypeStruct((slots, f_dim), bf16),
        jax.ShapeDtypeStruct((experts, feats), f32),
    )
    grads, hidden, router = pl.pallas_call(
        functools.partial(kernel, sections, n),
        out_shape=results,
        in_specs=[hbm] * 6,
        out_specs=(hbm,) * 3,
        scratch_shapes=[
            pltpu.VMEM((n, tokens, d_model), bf16),
            pltpu.VMEM((n, tokens + experts, LANES), bf16),
            pltpu.VMEM((n, tokens + experts, LANES), bf16),
            pltpu.VMEM((n, tiles, LANES), f32),
            pltpu.VMEM((tokens, d_model), bf16),
            pltpu.VMEM((experts, d_model), bf16),
            pltpu.VMEM((experts, LANES), bf16),
            pltpu.VMEM((tokens, d_model), bf16),
            pltpu.VMEM((experts, d_model), bf16),
            pltpu.VMEM((topk, tokens), jnp.int32),
            pltpu.VMEM((slots, f_dim), bf16),
            pltpu.VMEM((f_dim, d_model), bf16),
            pltpu.VMEM((tiles, experts, LANES), f32),
            pltpu.VMEM((tiles, LANES), f32),
            pltpu.VMEM((f_dim, slots), bf16),
            pltpu.VMEM((slots, total), bf16),
            pltpu.VMEM((tiles, f_dim, LANES), f32),
            pltpu.VMEM((tiles, f_dim, LANES), f32),
            pltpu.VMEM((f_dim, total), bf16),
            pltpu.VMEM((tiles, LANES), f32),
            pltpu.VMEM((tiles, experts, LANES), f32),
            pltpu.VMEM((tiles, experts, LANES), bf16),
            pltpu.VMEM((tokens, d_model), bf16),
            pltpu.VMEM((slots, f_dim), bf16),
            pltpu.VMEM((experts, feats), f32),
            dma((n, CHUNKS)),
            dma((n, CHUNKS, 5)),
            dma((ROWS_A,)),
            dma((2,)),
            dma((3,)),
            dma((3,)),
            dma((3,)),
            dma((9,)),
        ],
        compiler_params=pltpu.CompilerParams(
            collective_id=0, has_side_effects=True, vmem_limit_bytes=48 * 2**20
        ),
        cost_estimate=pl.CostEstimate(
            flops=2 * total * d_model * f_dim, bytes_accessed=4 * f_dim * d_model, transcendentals=0
        ),
    )(*(pltpu.with_memory_space_constraint(p, pltpu.HBM) for p in (og, x, rt, ids, hid, w)))
    return (grads[None], hidden[None, None], router.T[None])


def solution(mesh):
    placed = (
        P("section", "expert", None),
        P("section", "expert", None),
        P("section", None, None),
        P("section", "expert", None),
        P("section", "expert", None, None),
        P("section", "expert", None, None),
    )
    return jax.shard_map(
        functools.partial(shards, mesh.shape["section"], mesh.shape["expert"]),
        mesh=mesh,
        in_specs=placed,
        out_specs=(
            P("section", "expert", None),
            P("section", "expert", None, None),
            P("section", "expert", None),
        ),
        check_vma=False,
    )
```
